32 devices in a mesh: row: 2 (over x), col: 16 (over z, y, core).
Axes of the slice: x: 2, y: 2, z: 4, core: 2. Of those that a mesh axis runs over, the one named last changes fastest.
Arguments:
- activations: bfloat16 [32768, 896], P(('row', 'col')), may hold values from -6 to 6
- cotangent: bfloat16 [32768, 896], P(('row', 'col')), may hold values from -6 to 6
- inner_first: bfloat16 [14336, 1792], P('col', 'row'), may hold values from -6 to 6
- inner_second: bfloat16 [1792, 14336], P('row', 'col'), may hold values from -6 to 6
- outer_first: float32 [896, 1792], P('col', 'row'), may hold values from -6 to 6
- momentum_first: float32 [896, 1792], P('col', 'row'), may hold values from -3 to 3
- outer_second: float32 [896, 14336], P('row', 'col'), may hold values from -6 to 6
- momentum_second: float32 [896, 14336], P('row', 'col'), may hold values from -3 to 3
Outputs:
- new_outer_first: float32 [896, 1792], P('col', 'row')
- new_momentum_first: float32 [896, 1792], P('col', 'row')
- new_outer_second: float32 [896, 14336], P('row', 'col')
- new_momentum_second: float32 [896, 14336], P('row', 'col')
- reset_first: bfloat16 [14336, 1792], P('col', 'row')
- reset_second: bfloat16 [1792, 14336], P('row', 'col')
The draws below stay inside these ranges and needn't reach their ends.
All inputs are finite; a program needn't handle non-finite values.
Results may differ from the reference program's by a relative error of at most 0.003.
Values may be sent and summed in bfloat16 or wider, within the bound.
A program may use at most 64 MiB of HBM per device.

```python
import jax
import jax.numpy as jnp
from jax import lax

D = 896
TOK_DEV = 1024
TOKENS = 32768
N_ROW = 2
N_COL = 16


def block_levels(rng, dims, pieces, smallest, top_value):
    def one(position, shards_of):
        draws = jax.random.uniform(jax.random.fold_in(jax.random.fold_in(rng, 6), position), (shards_of,), jnp.float32, smallest / len(pieces), top_value / len(pieces))
        return jnp.repeat(jnp.exp(draws), dims[position] // shards_of).reshape((-1,) + (1,) * (len(dims) - position - 1))

    loudness = one(*pieces[0])
    for cut in pieces[1:]:
        loudness = loudness * one(*cut)
    return loudness


def centred(key, shape, spread, limit, pieces=(), held_as=jnp.bfloat16):
    drawn = jax.random.normal(key, shape, jnp.float32) * spread
    if len(pieces) > 0:
        drawn = block_levels(key, shape, pieces, -0.22, 0.18) * drawn
    return jnp.clip(drawn, min=-limit, max=limit).astype(held_as)


def setup_inputs(seed: int = 0) -> dict:
    arg_keys = jax.random.split(jax.random.key(seed), 9)
    activations = centred(arg_keys[0], (TOKENS, D), 1.0, 6.0, ((0, 32),))
    cotangent = centred(arg_keys[1], (TOKENS, D), 1.0, 6.0, ((0, 32),))
    inner_first = centred(arg_keys[2], (N_COL * D, N_ROW * D), 1.0, 6.0, ((0, 16), (1, 2)))
    inner_second = centred(arg_keys[3], (N_ROW * D, N_COL * D), 1.0, 6.0, ((0, 2), (1, 16)))
    outer_first = centred(arg_keys[4], (D, N_ROW * D), 1.0, 6.0, ((0, 16), (1, 2)), jnp.float32)
    momentum_first = centred(arg_keys[5], (D, N_ROW * D), 0.5, 3.0, ((0, 16), (1, 2)), jnp.float32)
    outer_second = centred(arg_keys[6], (D, N_COL * D), 1.0, 6.0, ((0, 2), (1, 16)), jnp.float32)
    momentum_second = centred(arg_keys[7], (D, N_COL * D), 0.5, 3.0, ((0, 2), (1, 16)), jnp.float32)
    return dict(activations=activations, cotangent=cotangent, inner_first=inner_first, inner_second=inner_second, outer_first=outer_first, momentum_first=momentum_first, outer_second=outer_second, momentum_second=momentum_second)


inner_rate = 1.0
outer_rate = 0.7
momentum_coef = 0.9

def path_step(inputs, grads, first_w, second_w):
    unit_scale = 1.0 / jnp.sqrt(jnp.float32(D))
    hidden = jnp.dot(inputs.astype(jnp.float32), first_w.astype(jnp.float32)) * unit_scale
    logistic = jax.nn.sigmoid(hidden)
    second_in = (hidden * logistic).astype(jnp.bfloat16)
    grad_second = jnp.dot(second_in.astype(jnp.float32).T, grads.astype(jnp.float32)) * unit_scale
    backward = jnp.dot(grads.astype(jnp.float32), second_w.astype(jnp.float32).T) * unit_scale
    first_cot = (backward * logistic * (1.0 + hidden * (1.0 - logistic))).astype(jnp.bfloat16)
    grad_first = jnp.dot(inputs.astype(jnp.float32).T, first_cot.astype(jnp.float32)) * unit_scale
    final_first = first_w.astype(jnp.float32) - inner_rate * grad_first
    final_second = second_w.astype(jnp.float32) - inner_rate * grad_second
    return (final_first, final_second)

def nesterov(outer_flat, moment_flat, summed, count):
    modules = summed.shape[0]
    outer_mods = outer_flat.reshape(D, modules, D).transpose(1, 0, 2)
    moment_mods = moment_flat.reshape(D, modules, D).transpose(1, 0, 2)
    pseudo_grad = outer_mods - summed / count
    moment_new = momentum_coef * moment_mods + pseudo_grad
    outer_new = outer_mods - outer_rate * (pseudo_grad + momentum_coef * moment_new)
    back_outer = outer_new.transpose(1, 0, 2).reshape(D, modules * D)
    back_moment = moment_new.transpose(1, 0, 2).reshape(D, modules * D)
    return (back_outer, back_moment)

def reference(activations, cotangent, inner_first, inner_second, outer_first, momentum_first, outer_second, momentum_second):

    def one_path(path, carry):
        sum_first, sum_second = carry
        path = jnp.asarray(path).astype(jnp.int32)
        grid_row = (path // N_COL).astype(jnp.int32)
        grid_col = (path % N_COL).astype(jnp.int32)
        zero = jnp.asarray(0).astype(jnp.int32)
        inputs = lax.dynamic_slice(activations, ((path * TOK_DEV).astype(jnp.int32), zero), (TOK_DEV, D))
        grads = lax.dynamic_slice(cotangent, ((path * TOK_DEV).astype(jnp.int32), zero), (TOK_DEV, D))
        first_w = lax.dynamic_slice(inner_first, ((grid_col * D).astype(jnp.int32), (grid_row * D).astype(jnp.int32)), (D, D))
        second_w = lax.dynamic_slice(inner_second, ((grid_row * D).astype(jnp.int32), (grid_col * D).astype(jnp.int32)), (D, D))
        final_first, final_second = path_step(inputs, grads, first_w, second_w)
        sum_first = sum_first.at[grid_row].add(final_first)
        sum_second = sum_second.at[grid_col].add(final_second)
        return (sum_first, sum_second)
    start = (jnp.zeros((N_ROW, D, D), jnp.float32), jnp.zeros((N_COL, D, D), jnp.float32))
    sum_first, sum_second = lax.fori_loop(0, N_ROW * N_COL, one_path, start)
    new_outer_first, new_momentum_first = nesterov(outer_first, momentum_first, sum_first, N_COL)
    new_outer_second, new_momentum_second = nesterov(outer_second, momentum_second, sum_second, N_ROW)
    reset_first = jnp.tile(new_outer_first.astype(jnp.bfloat16), (N_COL, 1))
    reset_second = jnp.tile(new_outer_second.astype(jnp.bfloat16), (N_ROW, 1))
    return (new_outer_first, new_momentum_first, new_outer_second, new_momentum_second, reset_first, reset_second)
```

```python
import functools

import jax
import jax.numpy as jnp
import numpy as np
from jax import lax
from jax.experimental import pallas as pl
from jax.experimental.pallas import tpu as pltpu
from jax.sharding import PartitionSpec as P

inner_rate = 1.0
outer_rate = 0.7
momentum_coef = 0.9


def nesterov(outer_rows, moment_rows, summed, count):
    pseudo_grad = outer_rows - summed / count
    moment_new = momentum_coef * moment_rows + pseudo_grad
    outer_new = outer_rows - outer_rate * (pseudo_grad + momentum_coef * moment_new)
    return (outer_new, moment_new)


def on_device_plain(
    activations,
    cotangent,
    inner_first,
    inner_second,
    outer_first,
    momentum_first,
    outer_second,
    momentum_second,
):
    width = inner_first.shape[0]
    unit_scale = 1.0 / jnp.sqrt(jnp.float32(width))
    row_count = lax.axis_size("row")
    col_count = lax.axis_size("col")
    rows_second = outer_second.shape[0]
    rows_first = outer_first.shape[0]
    hidden = jnp.dot(activations, inner_first, preferred_element_type=jnp.float32) * unit_scale
    logistic = jax.nn.sigmoid(hidden)
    second_in = (hidden * logistic).astype(jnp.bfloat16)
    backward = (
        lax.dot_general(
            cotangent, inner_second, (((1,), (1,)), ((), ())), preferred_element_type=jnp.float32
        )
        * unit_scale
    )
    first_cot = (backward * logistic * (1.0 + hidden * (1.0 - logistic))).astype(jnp.bfloat16)

    def final_rows(inputs, grads, weight):
        grad_rows = (
            lax.dot_general(
                inputs, grads, (((0,), (0,)), ((), ())), preferred_element_type=jnp.float32
            )
            * unit_scale
        )
        return weight.astype(jnp.float32) - inner_rate * grad_rows

    final_second = final_rows(second_in, cotangent, inner_second)
    summed_second = lax.psum(final_second, "row")
    final_first = final_rows(activations, first_cot, inner_first)
    summed_first = lax.psum(final_first, "col")
    mine_second = lax.dynamic_slice_in_dim(
        summed_second, lax.axis_index("row") * rows_second, rows_second, 0
    )
    mine_first = lax.dynamic_slice_in_dim(
        summed_first, lax.axis_index("col") * rows_first, rows_first, 0
    )
    new_outer_second, new_momentum_second = nesterov(
        outer_second, momentum_second, mine_second, row_count
    )
    new_outer_first, new_momentum_first = nesterov(
        outer_first, momentum_first, mine_first, col_count
    )
    reset_second = lax.all_gather(new_outer_second.astype(jnp.bfloat16), "row", axis=0, tiled=True)
    reset_first = lax.all_gather(new_outer_first.astype(jnp.bfloat16), "col", axis=0, tiled=True)
    return (
        new_outer_first,
        new_momentum_first,
        new_outer_second,
        new_momentum_second,
        reset_first,
        reset_second,
    )


MESH = pl.DeviceIdType.MESH
LANES = 128
TOKEN_TILE = 256
CHUNKS = 4
F32 = jnp.float32
BF16 = jnp.bfloat16


def pack_piece(piece, padded):
    rows, width = piece.shape
    blocks = [piece[:, j * LANES : (j + 1) * LANES] for j in range(width // LANES)]
    spare = padded - rows * len(blocks)
    if spare:
        blocks.append(jnp.zeros((spare, LANES), F32))
    return jnp.concatenate(blocks, axis=0)


def unpack_piece(packed, rows, width):
    return jnp.concatenate(
        [packed[j * rows : (j + 1) * rows] for j in range(width // LANES)], axis=1
    )


def outer_step_kernel(
    x_h,
    g_h,
    w1_h,
    w2_h,
    o1_h,
    m1_h,
    o2_h,
    m2_h,
    no1_h,
    nm1_h,
    no2_h,
    nm2_h,
    r1_h,
    r2_h,
    xv,
    gv,
    w1v,
    w2v,
    o1v,
    m1v,
    o2v,
    m2v,
    xt,
    st,
    dv,
    fc,
    f2,
    fsend,
    frecv,
    asend,
    arecv,
    f1,
    r1,
    s2,
    r2,
    own,
    na,
    nb,
    no1,
    nm1,
    no2,
    nm2,
    rs1,
    rs2,
    in_sem,
    out_sem,
    out2_sem,
    rs1_sem,
    fs_sem,
    fr_sem,
    as_sem,
    ar_sem,
    c1s_sem,
    c1r_sem,
    s2s_sem,
    s2r_sem,
    zs_sem,
    ys_sem,
    nar_sem,
    ks_sem,
    nbr_sem,
):
    row = lax.axis_index("row")
    col = lax.axis_index("col")
    n_col = lax.axis_size("col")
    chips = n_col // 2
    core = lax.rem(col, 2)
    chip = lax.div(col, 2)
    side = lax.rem(chip, 2)
    depth = lax.div(chip, 2)
    depths = chips // 2
    width = w1v.shape[0]
    tokens = xv.shape[0]
    half = o2v.shape[0]
    chunk = half // CHUNKS
    piece = o1v.shape[0]
    padded = s2.shape[1]
    scale = float(np.float32(1.0) / np.sqrt(np.float32(width)))

    across = (1 - row, col)
    sibling = (row, chip * 2 + 1 - core)

    def plane(other_chip):
        return (row, other_chip * 2 + core)

    loads = {}
    for i, (name, src, dst) in enumerate(
        (
            ("x", x_h, xv),
            ("w1", w1_h, w1v),
            ("g", g_h, gv),
            ("w2", w2_h, w2v),
            ("o2", o2_h, o2v),
            ("m2", m2_h, m2v),
            ("o1", o1_h, o1v),
            ("m1", m1_h, m1v),
        )
    ):
        loads[name] = pltpu.make_async_copy(src, dst, in_sem.at[i])
        loads[name].start()

    barrier = pltpu.get_barrier_semaphore()
    pl.semaphore_signal(barrier, inc=1, device_id=across, device_id_type=MESH)
    pl.semaphore_signal(barrier, inc=1, device_id=sibling, device_id_type=MESH)
    for d in range(1, chips):
        pl.semaphore_signal(
            barrier, inc=1, device_id=plane(lax.rem(chip + d, chips)), device_id_type=MESH
        )

    def remote(src, dst, send_sem, recv_sem, device):
        return pltpu.make_async_remote_copy(
            src_ref=src,
            dst_ref=dst,
            send_sem=send_sem,
            recv_sem=recv_sem,
            device_id=device,
            device_id_type=MESH,
        )

    loads["x"].wait()
    loads["w1"].wait()

    def forward(t, carry):
        at = pl.ds(pl.multiple_of(t * TOKEN_TILE, TOKEN_TILE), TOKEN_TILE)
        inputs = xv[at, :]
        hidden = jnp.dot(inputs, w1v[...], preferred_element_type=F32) * scale
        logistic = jax.nn.sigmoid(hidden)
        st[:, at] = (hidden * logistic).astype(BF16).T
        dv[at, :] = logistic * (1.0 + hidden * (1.0 - logistic))
        xt[:, at] = inputs.T
        return carry

    lax.fori_loop(0, tokens // TOKEN_TILE, forward, 0)
    loads["g"].wait()
    loads["w2"].wait()
    pl.semaphore_wait(barrier, chips + 1)

    mine = row * half
    theirs = (1 - row) * half

    def rows_of(base, i):
        return pl.ds(pl.multiple_of(base + i * chunk, 16), chunk)

    def part(i):
        return pl.ds(pl.multiple_of(i * chunk, 16), chunk)

    def final_second(base, i):
        at = rows_of(base, i)
        grad = jnp.dot(st[at, :], gv[...], preferred_element_type=F32) * scale
        final = w2v[at, :].astype(F32) - inner_rate * grad
        f2[at, :] = final
        return final

    def copy_final(i):
        return remote(fsend.at[part(i)], frecv.at[part(i)], fs_sem.at[i], fr_sem.at[i], across)

    def copy_partial(i):
        return remote(asend.at[part(i)], arecv.at[part(i)], as_sem.at[i], ar_sem.at[i], across)

    def send_final(i, carry):
        fsend[part(i), :] = final_second(theirs, i).astype(BF16)
        copy_final(i).start()
        return carry

    lax.fori_loop(0, CHUNKS // 2, send_final, 0)

    def backward(t, carry):
        at = pl.ds(pl.multiple_of(t * TOKEN_TILE, TOKEN_TILE), TOKEN_TILE)
        back = (
            lax.dot_general(
                gv[at, :], w2v[...], (((1,), (1,)), ((), ())), preferred_element_type=F32
            )
            * scale
        )
        fc[at, :] = (back * dv[at, :]).astype(BF16)
        return carry

    lax.fori_loop(0, tokens // TOKEN_TILE, backward, 0)

    def copy_core(t):
        at = pl.ds(t * 2, 2)
        return remote(
            f1.at[1 - core, at], r1.at[at], c1s_sem.at[t], c1r_sem.at[t], sibling
        )

    def final_first(t, carry):
        rows = 4 * piece
        at = pl.ds(pl.multiple_of(t * rows, 16), rows)
        grad = jnp.dot(xt[at, :], fc[...], preferred_element_type=F32) * scale
        final = w1v[at, :].astype(F32) - inner_rate * grad
        for j in range(4):
            f1[j % 2, t * 2 + j // 2] = final[j * piece : (j + 1) * piece]
        copy_core(t).start()
        return carry

    lax.fori_loop(0, chips // 2, final_first, 0)
    lax.fori_loop(CHUNKS // 2, CHUNKS, send_final, 0)

    def wait_core(t, carry):
        copy_core(t).wait_recv()
        return carry

    lax.fori_loop(0, chips // 2, wait_core, 0)

    def copy_sum(d):
        return remote(
            s2.at[d], r2.at[chip], s2s_sem.at[d], s2r_sem.at[chip], plane(lax.rem(chip + d, chips))
        )

    def send_sum(d, carry):
        owner = lax.rem(chip + d, chips)
        total = f1[core, owner] + r1[owner]
        s2[d] = pack_piece(total, padded).astype(BF16)
        copy_sum(d).start()
        return carry

    lax.fori_loop(1, chips, send_sum, 0)
    own[...] = pack_piece(f1[core, chip] + r1[chip], padded)

    loads["o2"].wait()
    loads["m2"].wait()

    def send_partial(i, carry):
        final = final_second(mine, i)
        share, _ = nesterov(o2v[part(i), :], m2v[part(i), :], final, 2)
        asend[part(i), :] = share.astype(BF16)
        copy_partial(i).start()
        return carry

    lax.fori_loop(0, CHUNKS, send_partial, 0)

    def out_second(i):
        return (
            pltpu.make_async_copy(no2.at[part(i)], no2_h.at[part(i)], out2_sem.at[0, i]),
            pltpu.make_async_copy(nm2.at[part(i)], nm2_h.at[part(i)], out2_sem.at[1, i]),
            pltpu.make_async_copy(
                rs2.at[rows_of(mine, i)], r2_h.at[rows_of(mine, i)], out2_sem.at[2, i]
            ),
        )

    def out_reset(i):
        at = rows_of(theirs, i)
        return pltpu.make_async_copy(rs2.at[at], r2_h.at[at], out2_sem.at[3, i])

    def take_final(i, carry):
        copy_final(i).wait_recv()
        summed = f2[rows_of(mine, i), :] + frecv[part(i), :].astype(F32)
        new_outer, new_moment = nesterov(o2v[part(i), :], m2v[part(i), :], summed, 2)
        no2[part(i), :] = new_outer
        nm2[part(i), :] = new_moment
        rs2[rows_of(mine, i), :] = new_outer.astype(BF16)
        for copy in out_second(i):
            copy.start()
        return carry

    lax.fori_loop(0, CHUNKS, take_final, 0)

    loads["o1"].wait()
    loads["m1"].wait()

    def take_sum(d, carry):
        source = lax.rem(chip + chips - d, chips)
        remote(
            s2.at[d], r2.at[source], s2s_sem.at[d], s2r_sem.at[source], plane(source)
        ).wait_recv()
        own[...] += r2[source].astype(F32)
        return carry

    lax.fori_loop(1, chips, take_sum, 0)
    summed = unpack_piece(own[...], piece, width)
    new_outer, new_moment = nesterov(o1v[...], m1v[...], summed, n_col)
    no1[...] = new_outer
    nm1[...] = new_moment
    na[chip] = pack_piece(new_outer, padded).astype(BF16)
    out_first = (
        pltpu.make_async_copy(no1, no1_h, out_sem.at[0]),
        pltpu.make_async_copy(nm1, nm1_h, out_sem.at[1]),
    )

    def copy_depth(d):
        other = lax.rem(depth + d, depths) * 2 + side
        return remote(na.at[chip], na.at[chip], zs_sem.at[d], nar_sem.at[chip], plane(other))

    def copy_side(d):
        held = lax.rem(depth + d, depths) * 2 + side
        return remote(
            na.at[held], na.at[held], ys_sem.at[d], nar_sem.at[held], plane(depth * 2 + 1 - side)
        )

    def copy_sibling(held):
        return remote(na.at[held], nb.at[held], ks_sem.at[held], nbr_sem.at[held], sibling)

    def wait_module(held):
        remote(
            na.at[held], na.at[held], ys_sem.at[0], nar_sem.at[held], plane(depth * 2 + 1 - side)
        ).wait_recv()

    for d in range(1, depths):
        copy_depth(d).start()
    copy_side(0).start()
    copy_sibling(chip).start()
    for copy in out_first:
        copy.start()

    def take_partial(i, carry):
        copy_partial(i).wait_recv()
        at = rows_of(theirs, i)
        share = (outer_rate * (1.0 + momentum_coef) / 2) * f2[at, :]
        rs2[at, :] = (arecv[part(i), :].astype(F32) + share).astype(BF16)
        out_reset(i).start()
        return carry

    lax.fori_loop(0, 2, take_partial, 0)

    def pass_on(d, carry):
        held = lax.rem(depth + d, depths) * 2 + side
        wait_module(held)
        copy_side(d).start()
        copy_sibling(held).start()
        return carry

    lax.fori_loop(1, depths, pass_on, 0)
    lax.fori_loop(2, CHUNKS - 1, take_partial, 0)

    def pass_core(d, carry):
        held = lax.rem(depth + d, depths) * 2 + 1 - side
        wait_module(held)
        copy_sibling(held).start()
        return carry

    lax.fori_loop(0, depths, pass_core, 0)

    def out_module(q):
        at = pl.ds(pl.multiple_of(q * 2 * piece, 16), 2 * piece)
        return pltpu.make_async_copy(rs1.at[at], r1_h.at[at], rs1_sem.at[q])

    def place(d, carry):
        q = lax.rem(chip + d, chips)
        remote(na.at[q], nb.at[q], ks_sem.at[q], nbr_sem.at[q], sibling).wait_recv()
        here = unpack_piece(na[q].astype(F32), piece, width)
        there = unpack_piece(nb[q].astype(F32), piece, width)
        both = jnp.concatenate(
            [jnp.where(core == 0, here, there), jnp.where(core == 0, there, here)], axis=0
        )
        rs1[pl.ds(pl.multiple_of(q * 2 * piece, 16), 2 * piece), :] = both.astype(BF16)
        out_module(q).start()
        return carry

    lax.fori_loop(0, chips, place, 0)
    lax.fori_loop(CHUNKS - 1, CHUNKS, take_partial, 0)

    def drain(i, carry):
        copy_final(i).wait_send()
        copy_partial(i).wait_send()
        for copy in out_second(i):
            copy.wait()
        out_reset(i).wait()
        return carry

    lax.fori_loop(0, CHUNKS, drain, 0)

    def drain_core(t, carry):
        copy_core(t).wait_send()
        return carry

    lax.fori_loop(0, chips // 2, drain_core, 0)
    for copy in out_first:
        copy.wait()
    for d in range(1, chips):
        copy_sum(d).wait_send()
    for d in range(depths):
        copy_side(d).wait_send()
        if d:
            copy_depth(d).wait_send()
    for q in range(chips):
        copy_sibling(q).wait_send()
        out_module(q).wait()


def on_device_fused(
    activations,
    cotangent,
    inner_first,
    inner_second,
    outer_first,
    momentum_first,
    outer_second,
    momentum_second,
):
    tokens, width = activations.shape
    piece = outer_first.shape[0]
    half = outer_second.shape[0]
    chips = lax.axis_size("col") // 2
    padded = -(-piece * (width // LANES) // 16) * 16
    anywhere = pl.BlockSpec(memory_space=pl.ANY)
    dma = pltpu.SemaphoreType.DMA
    return pl.pallas_call(
        outer_step_kernel,
        out_shape=(
            jax.ShapeDtypeStruct((piece, width), F32),
            jax.ShapeDtypeStruct((piece, width), F32),
            jax.ShapeDtypeStruct((half, width), F32),
            jax.ShapeDtypeStruct((half, width), F32),
            jax.ShapeDtypeStruct((width, width), BF16),
            jax.ShapeDtypeStruct((width, width), BF16),
        ),
        in_specs=[anywhere] * 8,
        out_specs=[anywhere] * 6,
        scratch_shapes=[
            pltpu.VMEM((tokens, width), BF16),
            pltpu.VMEM((tokens, width), BF16),
            pltpu.VMEM((width, width), BF16),
            pltpu.VMEM((width, width), BF16),
            pltpu.VMEM((piece, width), F32),
            pltpu.VMEM((piece, width), F32),
            pltpu.VMEM((half, width), F32),
            pltpu.VMEM((half, width), F32),
            pltpu.VMEM((width, tokens), BF16),
            pltpu.VMEM((width, tokens), BF16),
            pltpu.VMEM((tokens, width), F32),
            pltpu.VMEM((tokens, width), BF16),
            pltpu.VMEM((width, width), F32),
            pltpu.VMEM((half, width), BF16),
            pltpu.VMEM((half, width), BF16),
            pltpu.VMEM((half, width), BF16),
            pltpu.VMEM((half, width), BF16),
            pltpu.VMEM((2, chips, piece, width), F32),
            pltpu.VMEM((chips, piece, width), F32),
            pltpu.VMEM((chips, padded, LANES), BF16),
            pltpu.VMEM((chips, padded, LANES), BF16),
            pltpu.VMEM((padded, LANES), F32),
            pltpu.VMEM((chips, padded, LANES), BF16),
            pltpu.VMEM((chips, padded, LANES), BF16),
            pltpu.VMEM((piece, width), F32),
            pltpu.VMEM((piece, width), F32),
            pltpu.VMEM((half, width), F32),
            pltpu.VMEM((half, width), F32),
            pltpu.VMEM((width, width), BF16),
            pltpu.VMEM((width, width), BF16),
            dma((8,)),
            dma((2,)),
            dma((4, CHUNKS)),
            dma((chips,)),
            dma((CHUNKS,)),
            dma((CHUNKS,)),
            dma((CHUNKS,)),
            dma((CHUNKS,)),
            dma((chips // 2,)),
            dma((chips // 2,)),
            dma((chips,)),
            dma((chips,)),
            dma((chips // 2,)),
            dma((chips // 2,)),
            dma((chips,)),
            dma((chips,)),
            dma((chips,)),
        ],
        compiler_params=pltpu.CompilerParams(
            collective_id=0, has_side_effects=True, vmem_limit_bytes=60 * 1024 * 1024
        ),
        cost_estimate=pl.CostEstimate(
            flops=8 * tokens * width * width,
            bytes_accessed=17_000_000,
            transcendentals=tokens * width,
        ),
    )(
        activations,
        cotangent,
        inner_first,
        inner_second,
        outer_first,
        momentum_first,
        outer_second,
        momentum_second,
    )


def on_device(mesh):
    if mesh.shape["row"] == 2 and mesh.shape["col"] == 16:
        return on_device_fused
    return on_device_plain


def solution(mesh):
    return jax.shard_map(
        on_device(mesh),
        mesh=mesh,
        in_specs=(
            P(("row", "col"), None),
            P(("row", "col"), None),
            P("col", "row"),
            P("row", "col"),
            P("col", "row"),
            P("col", "row"),
            P("row", "col"),
            P("row", "col"),
        ),
        out_specs=(
            P("col", "row"),
            P("col", "row"),
            P("row", "col"),
            P("row", "col"),
            P("col", "row"),
            P("row", "col"),
        ),
        check_vma=False,
    )
```

```python
import functools

import jax
import jax.numpy as jnp
import numpy as np
from jax import lax
from jax.experimental import pallas as pl
from jax.experimental.pallas import tpu as pltpu
from jax.sharding import PartitionSpec as P

inner_rate = 1.0
outer_rate = 0.7
momentum_coef = 0.9


def nesterov(outer_rows, moment_rows, summed, count):
    pseudo_grad = outer_rows - summed / count
    moment_new = momentum_coef * moment_rows + pseudo_grad
    outer_new = outer_rows - outer_rate * (pseudo_grad + momentum_coef * moment_new)
    return (outer_new, moment_new)


def on_device_plain(
    activations,
    cotangent,
    inner_first,
    inner_second,
    outer_first,
    momentum_first,
    outer_second,
    momentum_second,
):
    width = inner_first.shape[0]
    unit_scale = 1.0 / jnp.sqrt(jnp.float32(width))
    row_count = lax.axis_size("row")
    col_count = lax.axis_size("col")
    rows_second = outer_second.shape[0]
    rows_first = outer_first.shape[0]
    hidden = jnp.dot(activations, inner_first, preferred_element_type=jnp.float32) * unit_scale
    logistic = jax.nn.sigmoid(hidden)
    second_in = (hidden * logistic).astype(jnp.bfloat16)
    backward = (
        lax.dot_general(
            cotangent, inner_second, (((1,), (1,)), ((), ())), preferred_element_type=jnp.float32
        )
        * unit_scale
    )
    first_cot = (backward * logistic * (1.0 + hidden * (1.0 - logistic))).astype(jnp.bfloat16)

    def final_rows(inputs, grads, weight):
        grad_rows = (
            lax.dot_general(
                inputs, grads, (((0,), (0,)), ((), ())), preferred_element_type=jnp.float32
            )
            * unit_scale
        )
        return weight.astype(jnp.float32) - inner_rate * grad_rows

    final_second = final_rows(second_in, cotangent, inner_second)
    summed_second = lax.psum(final_second, "row")
    final_first = final_rows(activations, first_cot, inner_first)
    summed_first = lax.psum(final_first, "col")
    mine_second = lax.dynamic_slice_in_dim(
        summed_second, lax.axis_index("row") * rows_second, rows_second, 0
    )
    mine_first = lax.dynamic_slice_in_dim(
        summed_first, lax.axis_index("col") * rows_first, rows_first, 0
    )
    new_outer_second, new_momentum_second = nesterov(
        outer_second, momentum_second, mine_second, row_count
    )
    new_outer_first, new_momentum_first = nesterov(
        outer_first, momentum_first, mine_first, col_count
    )
    reset_second = lax.all_gather(new_outer_second.astype(jnp.bfloat16), "row", axis=0, tiled=True)
    reset_first = lax.all_gather(new_outer_first.astype(jnp.bfloat16), "col", axis=0, tiled=True)
    return (
        new_outer_first,
        new_momentum_first,
        new_outer_second,
        new_momentum_second,
        reset_first,
        reset_second,
    )


MESH = pl.DeviceIdType.MESH
LANES = 128
TOKEN_TILE = 256
CHUNKS = 4
F32 = jnp.float32
BF16 = jnp.bfloat16


def pack_piece(piece, padded):
    rows, width = piece.shape
    blocks = [piece[:, j * LANES : (j + 1) * LANES] for j in range(width // LANES)]
    spare = padded - rows * len(blocks)
    if spare:
        blocks.append(jnp.zeros((spare, LANES), F32))
    return jnp.concatenate(blocks, axis=0)


def unpack_piece(packed, rows, width):
    return jnp.concatenate(
        [packed[j * rows : (j + 1) * rows] for j in range(width // LANES)], axis=1
    )


def outer_step_kernel(
    x_h,
    g_h,
    w1_h,
    w2_h,
    o1_h,
    m1_h,
    o2_h,
    m2_h,
    no1,
    nm1,
    no2,
    nm2,
    rs1,
    rs2,
    xv,
    gv,
    w1v,
    w2v,
    o1v,
    m1v,
    o2v,
    m2v,
    xt,
    st,
    dv,
    fc,
    f2,
    fsend,
    frecv,
    asend,
    arecv,
    f1,
    r1,
    s2,
    r2,
    own,
    na,
    nb,
    in_sem,
    x_sem,
    fs_sem,
    fr_sem,
    as_sem,
    ar_sem,
    c1s_sem,
    c1r_sem,
    s2s_sem,
    s2r_sem,
    zs_sem,
    ys_sem,
    nar_sem,
    ks_sem,
    nbr_sem,
):
    row = lax.axis_index("row")
    col = lax.axis_index("col")
    n_col = lax.axis_size("col")
    chips = n_col // 2
    core = lax.rem(col, 2)
    chip = lax.div(col, 2)
    side = lax.rem(chip, 2)
    depth = lax.div(chip, 2)
    depths = chips // 2
    width = w1v.shape[0]
    tokens = xv.shape[0]
    half = o2v.shape[0]
    chunk = half // CHUNKS
    piece = o1v.shape[0]
    padded = s2.shape[1]
    scale = float(np.float32(1.0) / np.sqrt(np.float32(width)))

    across = (1 - row, col)
    sibling = (row, chip * 2 + 1 - core)

    def plane(other_chip):
        return (row, other_chip * 2 + core)

    tiles = tokens // TOKEN_TILE

    def tile_of(t):
        return pl.ds(pl.multiple_of(t * TOKEN_TILE, TOKEN_TILE), TOKEN_TILE)

    def load_tokens(t):
        return pltpu.make_async_copy(x_h.at[tile_of(t)], xv.at[tile_of(t)], x_sem.at[t])

    loads = {
        name: pltpu.make_async_copy(src, dst, in_sem.at[i])
        for i, (name, src, dst) in enumerate(
            (
                ("w1", w1_h, w1v),
                ("g", g_h, gv),
                ("w2", w2_h, w2v),
                ("o2", o2_h, o2v),
                ("m2", m2_h, m2v),
                ("o1", o1_h, o1v),
                ("m1", m1_h, m1v),
            )
        )
    }
    loads["w1"].start()
    for t in range(tiles):
        load_tokens(t).start()

    barrier = pltpu.get_barrier_semaphore()
    pl.semaphore_signal(barrier, inc=1, device_id=across, device_id_type=MESH)
    pl.semaphore_signal(barrier, inc=1, device_id=sibling, device_id_type=MESH)
    for d in range(1, chips):
        pl.semaphore_signal(
            barrier, inc=1, device_id=plane(lax.rem(chip + d, chips)), device_id_type=MESH
        )

    def remote(src, dst, send_sem, recv_sem, device):
        return pltpu.make_async_remote_copy(
            src_ref=src,
            dst_ref=dst,
            send_sem=send_sem,
            recv_sem=recv_sem,
            device_id=device,
            device_id_type=MESH,
        )

    mine = row * half
    theirs = (1 - row) * half
    first = LANES
    rest = (half - first) // 2

    def sent_part(sender, i):
        if i == 0:
            return (1 - sender) * (half - first), first
        return sender * first + (i - 1) * rest, rest

    def rows_at(start, size):
        return pl.ds(pl.multiple_of(start, 16), size)

    def hidden_of(inputs, weight):
        hidden = jnp.dot(inputs, weight, preferred_element_type=F32) * scale
        return hidden, jax.nn.sigmoid(hidden)

    loads["w1"].wait()
    start = theirs + sent_part(row, 0)[0]
    early = pl.ds(pl.multiple_of(start, LANES), first)

    def forward_early(t, carry):
        load_tokens(t).wait()
        hidden, logistic = hidden_of(xv[tile_of(t), :], w1v[:, early])
        st[early, tile_of(t)] = (hidden * logistic).astype(BF16).T
        return carry

    loads["g"].start()
    loads["w2"].start()
    lax.fori_loop(0, tiles, forward_early, 0)
    loads["g"].wait()
    loads["w2"].wait()
    for name in ("o2", "m2", "o1", "m1"):
        loads[name].start()
    pl.semaphore_wait(barrier, chips + 1)

    def part(i):
        return pl.ds(pl.multiple_of(i * chunk, 16), chunk)

    def final_second(at):
        grad = jnp.dot(st[at, :], gv[...], preferred_element_type=F32) * scale
        final = w2v[at, :].astype(F32) - inner_rate * grad
        f2[at, :] = final
        return final

    def copy_final(i):
        at = rows_at(*sent_part(row, i))
        return remote(fsend.at[at], frecv.at[at], fs_sem.at[i], fr_sem.at[i], across)

    def copy_partial(i):
        return remote(asend.at[part(i)], arecv.at[part(i)], as_sem.at[i], ar_sem.at[i], across)

    def send_final(i):
        start, size = sent_part(row, i)
        fsend[rows_at(start, size), :] = final_second(rows_at(theirs + start, size)).astype(BF16)
        copy_final(i).start()

    send_final(0)

    def forward(t, carry):
        at = tile_of(t)
        inputs = xv[at, :]
        hidden, logistic = hidden_of(inputs, w1v[...])
        st[:, at] = (hidden * logistic).astype(BF16).T
        dv[at, :] = logistic * (1.0 + hidden * (1.0 - logistic))
        xt[:, at] = inputs.T
        return carry

    lax.fori_loop(0, tiles, forward, 0)
    send_final(1)

    def backward(t, carry):
        at = tile_of(t)
        back = (
            lax.dot_general(
                gv[at, :], w2v[...], (((1,), (1,)), ((), ())), preferred_element_type=F32
            )
            * scale
        )
        fc[at, :] = (back * dv[at, :]).astype(BF16)
        return carry

    lax.fori_loop(0, tiles, backward, 0)

    def copy_core(t):
        at = pl.ds(t * 2, 2)
        return remote(
            f1.at[1 - core, at], r1.at[at], c1s_sem.at[t], c1r_sem.at[t], sibling
        )

    def copy_sum(owner):
        return remote(
            s2.at[owner], r2.at[chip], s2s_sem.at[owner], s2r_sem.at[chip], plane(owner)
        )

    def chip_sum(owner):
        return pack_piece(f1[core, owner] + r1[owner], padded)

    def send_sum(owner):
        s2[owner] = chip_sum(owner).astype(BF16)
        copy_sum(owner).start()

    def final_first(turn):
        t = lax.rem(depth + 1 + turn, depths)
        rows = 4 * piece
        at = pl.ds(pl.multiple_of(t * rows, 16), rows)
        grad = jnp.dot(xt[at, :], fc[...], preferred_element_type=F32) * scale
        final = w1v[at, :].astype(F32) - inner_rate * grad
        for j in range(4):
            f1[j % 2, t * 2 + j // 2] = final[j * piece : (j + 1) * piece]
        copy_core(t).start()

    def pass_sums(turn):
        t = lax.rem(depth + 1 + turn, depths)
        copy_core(t).wait_recv()
        send_sum(t * 2 + side)
        send_sum(t * 2 + 1 - side)

    def first_turn(turn, carry):
        final_first(turn)
        pass_sums(turn - 1)
        return carry

    final_first(0)
    lax.fori_loop(1, depths, first_turn, 0)
    send_final(2)
    copy_core(depth).wait_recv()
    send_sum(depth * 2 + 1 - side)
    own[...] = chip_sum(chip)

    loads["o2"].wait()
    loads["m2"].wait()

    def send_partial(i, carry):
        final = final_second(rows_at(mine + i * chunk, chunk))
        share, _ = nesterov(o2v[part(i), :], m2v[part(i), :], final, 2)
        asend[part(i), :] = share.astype(BF16)
        copy_partial(i).start()
        return carry

    lax.fori_loop(0, CHUNKS, send_partial, 0)

    def take_final(i):
        start, size = sent_part(1 - row, i)
        at, there = rows_at(start, size), rows_at(mine + start, size)
        remote(
            fsend.at[at], frecv.at[at], fs_sem.at[i], fr_sem.at[i], across
        ).wait_recv()
        summed = f2[there, :] + frecv[at, :].astype(F32)
        new_outer, new_moment = nesterov(o2v[at, :], m2v[at, :], summed, 2)
        no2[at, :] = new_outer
        nm2[at, :] = new_moment
        rs2[there, :] = new_outer.astype(BF16)

    for i in range(3):
        take_final(i)

    def take_partial(i, carry):
        copy_partial(i).wait_recv()
        at = rows_at(theirs + i * chunk, chunk)
        share = (outer_rate * (1.0 + momentum_coef) / 2) * f2[at, :]
        rs2[at, :] = (arecv[part(i), :].astype(F32) + share).astype(BF16)
        return carry

    lax.fori_loop(0, 1, take_partial, 0)

    loads["o1"].wait()
    loads["m1"].wait()

    def take_sum(d, carry):
        source = lax.rem(chip + chips - d, chips)
        remote(
            s2.at[source], r2.at[source], s2s_sem.at[source], s2r_sem.at[source], plane(source)
        ).wait_recv()
        own[...] += r2[source].astype(F32)
        return carry

    lax.fori_loop(1, chips, take_sum, 0)
    summed = unpack_piece(own[...], piece, width)
    new_outer, new_moment = nesterov(o1v[...], m1v[...], summed, n_col)
    no1[...] = new_outer
    nm1[...] = new_moment
    na[chip] = pack_piece(new_outer, padded).astype(BF16)

    def copy_depth(d):
        other = lax.rem(depth + d, depths) * 2 + side
        return remote(na.at[chip], na.at[chip], zs_sem.at[d], nar_sem.at[chip], plane(other))

    def copy_side(d):
        held = lax.rem(depth + d, depths) * 2 + side
        return remote(
            na.at[held], na.at[held], ys_sem.at[d], nar_sem.at[held], plane(depth * 2 + 1 - side)
        )

    def copy_sibling(held):
        return remote(na.at[held], nb.at[held], ks_sem.at[held], nbr_sem.at[held], sibling)

    def wait_module(held):
        remote(
            na.at[held], na.at[held], ys_sem.at[0], nar_sem.at[held], plane(depth * 2 + 1 - side)
        ).wait_recv()

    for d in range(1, depths):
        copy_depth(d).start()
    copy_side(0).start()
    copy_sibling(chip).start()
    lax.fori_loop(1, 2, take_partial, 0)

    def pass_on(d, carry):
        held = lax.rem(depth + d, depths) * 2 + side
        wait_module(held)
        copy_side(d).start()
        copy_sibling(held).start()
        return carry

    lax.fori_loop(1, depths, pass_on, 0)
    lax.fori_loop(2, CHUNKS - 1, take_partial, 0)

    def pass_core(d, carry):
        held = lax.rem(depth + d, depths) * 2 + 1 - side
        wait_module(held)
        copy_sibling(held).start()
        return carry

    lax.fori_loop(0, depths, pass_core, 0)

    def place(d, carry):
        q = lax.rem(chip + d, chips)
        remote(na.at[q], nb.at[q], ks_sem.at[q], nbr_sem.at[q], sibling).wait_recv()
        here = unpack_piece(na[q].astype(F32), piece, width)
        there = unpack_piece(nb[q].astype(F32), piece, width)
        both = jnp.concatenate(
            [jnp.where(core == 0, here, there), jnp.where(core == 0, there, here)], axis=0
        )
        rs1[pl.ds(pl.multiple_of(q * 2 * piece, 16), 2 * piece), :] = both.astype(BF16)
        return carry

    lax.fori_loop(0, chips, place, 0)
    lax.fori_loop(CHUNKS - 1, CHUNKS, take_partial, 0)

    for i in range(3):
        copy_final(i).wait_send()

    def drain(i, carry):
        copy_partial(i).wait_send()
        return carry

    lax.fori_loop(0, CHUNKS, drain, 0)

    def drain_core(t, carry):
        copy_core(t).wait_send()
        return carry

    lax.fori_loop(0, depths, drain_core, 0)
    for d in range(1, chips):
        copy_sum(lax.rem(chip + d, chips)).wait_send()
    for d in range(depths):
        copy_side(d).wait_send()
        if d:
            copy_depth(d).wait_send()
    for q in range(chips):
        copy_sibling(q).wait_send()


def write_kernel(*refs):
    count = (len(refs) - 1) // 2
    copies = [
        pltpu.make_async_copy(refs[i], refs[count + i], refs[-1].at[i]) for i in range(count)
    ]
    for copy in copies:
        copy.start()
    for copy in copies:
        copy.wait()


def on_device_fused(
    activations,
    cotangent,
    inner_first,
    inner_second,
    outer_first,
    momentum_first,
    outer_second,
    momentum_second,
):
    tokens, width = activations.shape
    piece = outer_first.shape[0]
    half = outer_second.shape[0]
    chips = lax.axis_size("col") // 2
    padded = -(-piece * (width // LANES) // 16) * 16
    anywhere = pl.BlockSpec(memory_space=pl.ANY)
    dma = pltpu.SemaphoreType.DMA
    shapes = (
        ((piece, width), F32),
        ((piece, width), F32),
        ((half, width), F32),
        ((half, width), F32),
        ((width, width), BF16),
        ((width, width), BF16),
    )
    held = pl.BlockSpec(memory_space=pltpu.VMEM)
    results = pl.pallas_call(
        outer_step_kernel,
        out_shape=tuple(pltpu.VMEM(shape, dtype) for shape, dtype in shapes),
        in_specs=[anywhere] * 8,
        out_specs=[held] * 6,
        scratch_shapes=[
            pltpu.VMEM((tokens, width), BF16),
            pltpu.VMEM((tokens, width), BF16),
            pltpu.VMEM((width, width), BF16),
            pltpu.VMEM((width, width), BF16),
            pltpu.VMEM((piece, width), F32),
            pltpu.VMEM((piece, width), F32),
            pltpu.VMEM((half, width), F32),
            pltpu.VMEM((half, width), F32),
            pltpu.VMEM((width, tokens), BF16),
            pltpu.VMEM((width, tokens), BF16),
            pltpu.VMEM((tokens, width), F32),
            pltpu.VMEM((tokens, width), BF16),
            pltpu.VMEM((width, width), F32),
            pltpu.VMEM((half, width), BF16),
            pltpu.VMEM((half, width), BF16),
            pltpu.VMEM((half, width), BF16),
            pltpu.VMEM((half, width), BF16),
            pltpu.VMEM((2, chips, piece, width), F32),
            pltpu.VMEM((chips, piece, width), F32),
            pltpu.VMEM((chips, padded, LANES), BF16),
            pltpu.VMEM((chips, padded, LANES), BF16),
            pltpu.VMEM((padded, LANES), F32),
            pltpu.VMEM((chips, padded, LANES), BF16),
            pltpu.VMEM((chips, padded, LANES), BF16),
            dma((8,)),
            dma((tokens // TOKEN_TILE,)),
            dma((3,)),
            dma((3,)),
            dma((CHUNKS,)),
            dma((CHUNKS,)),
            dma((chips // 2,)),
            dma((chips // 2,)),
            dma((chips,)),
            dma((chips,)),
            dma((chips // 2,)),
            dma((chips // 2,)),
            dma((chips,)),
            dma((chips,)),
            dma((chips,)),
        ],
        compiler_params=pltpu.CompilerParams(
            collective_id=0, has_side_effects=True, vmem_limit_bytes=50 * 1024 * 1024
        ),
        cost_estimate=pl.CostEstimate(
            flops=8 * tokens * width * width,
            bytes_accessed=17_000_000,
            transcendentals=tokens * width,
        ),
    )(
        activations,
        cotangent,
        inner_first,
        inner_second,
        outer_first,
        momentum_first,
        outer_second,
        momentum_second,
    )
    return pl.pallas_call(
        write_kernel,
        out_shape=tuple(jax.ShapeDtypeStruct(shape, dtype) for shape, dtype in shapes),
        in_specs=[held] * 6,
        out_specs=[anywhere] * 6,
        scratch_shapes=[dma((6,))],
    )(*results)


def on_device(mesh):
    if mesh.shape["row"] == 2 and mesh.shape["col"] == 16:
        return on_device_fused
    return on_device_plain


def solution(mesh):
    return jax.shard_map(
        on_device(mesh),
        mesh=mesh,
        in_specs=(
            P(("row", "col"), None),
            P(("row", "col"), None),
            P("col", "row"),
            P("row", "col"),
            P("col", "row"),
            P("col", "row"),
            P("row", "col"),
            P("row", "col"),
        ),
        out_specs=(
            P("col", "row"),
            P("col", "row"),
            P("row", "col"),
            P("row", "col"),
            P("col", "row"),
            P("row", "col"),
        ),
        check_vma=False,
    )
```
